32 devices in a mesh: row: 8 (over z, y), col: 4 (over x, core).
Axes of the slice: x: 2, y: 2, z: 4, core: 2. Of those that a mesh axis runs over, the one named last changes fastest.
Arguments:
- blocks: float32 [32, 384, 2048], P(('row', 'col')), may hold values from -1.2 to 1.2
- eps_occ: float32 [32], replicated, may hold values from -3 to -0.3
- eps_vir: float32 [384], replicated, may hold values from 0.1 to 3
- partner: int32 [2, 32], replicated, may hold values from 0 to 31, as said below
Outputs:
- gamma: float32 [32, 384, 2048], P(('row', 'col'))
- density: float32 [384, 384], P('row', 'col')
The draws below stay inside these ranges and needn't reach their ends.
Inputs may be any that keep to these rules, and one draw needn't show every extreme that they name: Orbital index = row index * 4 + col index. In each round the partner of orbital (r, c) is (sigma_t(r), tau_t(c)), where sigma_t and tau_t are pairings without fixed points of the row indices and of the col indices; so partner[t, partner[t, i]] = i and partner[t, i] != i.
All inputs are finite; a program needn't handle non-finite values.
Results may differ from the reference program's by a relative error of at most 0.0003.
Values sent between devices are 32-bit elements; how exact they have to be, the bound alone decides.
A program may use at most 128 MiB of HBM per device.

```python
import jax
import jax.numpy as jnp
from jax import lax

VIR = 384
AUX = 2048
ROUNDS = 2
OCC = 32
N_ROW = 8
N_COL = 4


def pairing(key, count):
    order = jax.random.permutation(key, count).astype(jnp.int32)
    mates = order.reshape(-1, 2)[:, ::-1].reshape(-1)
    return jnp.zeros((count,), jnp.int32).at[order].set(mates)


def draw_partner(key, part):
    rounds_list = []
    for step_index in range(ROUNDS):
        sigma = pairing(jax.random.fold_in(key, 2 * step_index + 11), N_ROW)
        tau = pairing(jax.random.fold_in(key, 2 * step_index + 12), N_COL)
        grid = sigma[:, None] * N_COL + tau[None, :]
        rounds_list.append(grid.reshape(-1))
    return jnp.stack(rounds_list).astype(jnp.int32)


def steps_of(stream_key, shape, shards, smallest, largest):
    def one(dim, blocks):
        steps = jax.random.uniform(jax.random.fold_in(jax.random.fold_in(stream_key, 6), dim), (blocks,), jnp.float32, smallest / len(shards), largest / len(shards))
        return jnp.repeat(jnp.exp(steps), shape[dim] // blocks).reshape((-1,) + (1,) * (len(shape) - dim - 1))

    gain = one(*shards[0])
    for cut in shards[1:]:
        gain = gain * one(*cut)
    return gain


def noise(own_key, shape, width, limit, split=(), kind=jnp.bfloat16):
    entries = jax.random.normal(own_key, shape, jnp.float32) * width
    if len(split) > 0:
        entries = steps_of(own_key, shape, split, -0.22, 0.18) * entries
    return jnp.clip(entries, min=-limit, max=limit).astype(kind)


def setup_inputs(seed: int = 0) -> dict:
    arg_keys = jax.random.split(jax.random.key(seed), 5)
    blocks = noise(arg_keys[0], (OCC, VIR, AUX), 0.2, 1.2, ((0, 32),), jnp.float32)
    eps_occ = jnp.clip(jax.random.uniform(arg_keys[1], (OCC,), jnp.float32, -3.0, -0.3), -3.0, -0.3)
    eps_vir = jnp.clip(jax.random.uniform(arg_keys[2], (VIR,), jnp.float32, 0.1, 3.0), 0.1, 3.0)
    partner = draw_partner(jax.random.fold_in(arg_keys[4], 71), 0)
    return dict(blocks=blocks, eps_occ=eps_occ, eps_vir=eps_vir, partner=partner)


def pair_terms(own_block, mate_block, energy_own, energy_mate, eps_vir):
    pairs = jnp.dot(own_block, mate_block.T, precision=lax.Precision.HIGHEST, preferred_element_type=jnp.float32)
    denom = eps_vir[:, None] + eps_vir[None, :] - energy_own - energy_mate
    amp = -pairs / denom
    tamp = 2.0 * amp - amp.T
    gamma_term = jnp.dot(tamp, mate_block, precision=lax.Precision.HIGHEST, preferred_element_type=jnp.float32)
    dens_term = jnp.dot(amp, tamp.T, precision=lax.Precision.HIGHEST, preferred_element_type=jnp.float32)
    return gamma_term, dens_term


def reference(blocks, eps_occ, eps_vir, partner):
    def one_orbital(orbital):
        own_block = lax.dynamic_index_in_dim(blocks, orbital, 0, keepdims=False)
        energy_own = lax.dynamic_index_in_dim(eps_occ, orbital, 0, keepdims=False)
        gamma_sum = jnp.zeros((VIR, AUX), jnp.float32)
        dens_sum = jnp.zeros((VIR, VIR), jnp.float32)
        for step_index in range(ROUNDS):
            mate = lax.dynamic_index_in_dim(partner[step_index], orbital, 0, keepdims=False).astype(jnp.int32)
            mate_block = lax.dynamic_index_in_dim(blocks, mate, 0, keepdims=False)
            energy_mate = lax.dynamic_index_in_dim(eps_occ, mate, 0, keepdims=False)
            gamma_term, dens_term = pair_terms(own_block, mate_block, energy_own, energy_mate, eps_vir)
            gamma_sum = gamma_sum + gamma_term
            dens_sum = dens_sum + dens_term
        return gamma_sum, dens_sum

    gamma, dens_all = lax.map(one_orbital, jnp.arange(OCC, dtype=jnp.int32))
    density = jnp.sum(dens_all, axis=0) / jnp.float32(OCC)
    return gamma, density
```

```python
import functools

import jax
import jax.numpy as jnp
from jax import lax
from jax.experimental import pallas as pl
from jax.experimental.pallas import tpu as pltpu
from jax.sharding import PartitionSpec as P

MESH = pl.DeviceIdType.MESH
CHUNKS = 8
DOT = lax.Precision.HIGH


def exchange_kernel(n_row, n_col, rounds, chunks, partner_ref, own_ref, mate_ref, *scratch):
    lines, sels, fwds = scratch[:chunks], scratch[chunks : 2 * chunks], scratch[2 * chunks : 3 * chunks]
    s1s, s1r, s2s, s2r, s3s, s3r, s4s, s4r, local1, local4 = scratch[3 * chunks :]
    nz, plane = n_row // 2, 2 * n_col
    half = nz // 2
    deep = own_ref.shape[0] // 2
    rows, width = deep // chunks, own_ref.shape[1] // n_col
    row, col = lax.axis_index("row"), lax.axis_index("col")
    z, y = row // 2, row % 2
    p = y * n_col + col
    upper = z // half
    hub_near = half - 1 + upper
    hub_far = half - upper
    is_hub = z == hub_near

    def device(zz, q):
        return (zz * 2 + q // n_col, q % n_col)

    def piece(q, k):
        return (
            pl.ds(pl.multiple_of(q // n_col * deep + k * rows, 8), rows),
            pl.ds(pl.multiple_of(q % n_col * width, 128), width),
        )

    def block(zz):
        return pl.ds(zz * plane, plane)

    def spread(k, o):
        q = lax.rem(p + o, plane)
        return pltpu.make_async_remote_copy(
            src_ref=own_ref.at[piece(q, k)],
            dst_ref=lines[k].at[z * plane + p],
            send_sem=s1s.at[k, o],
            recv_sem=s1r.at[k, o],
            device_id=device(z, q),
            device_id_type=MESH,
        )

    def spread_own(k):
        return pltpu.make_async_copy(own_ref.at[piece(p, k)], lines[k].at[z * plane + p], local1.at[k])

    def to_hub(k, slot, hub):
        return pltpu.make_async_remote_copy(
            src_ref=lines[k].at[block(z)],
            dst_ref=lines[k].at[block(z)],
            send_sem=s2s.at[k, slot],
            recv_sem=s2r.at[k, z],
            device_id=device(hub, p),
            device_id_type=MESH,
        )

    def from_z(k, zz):
        return pltpu.make_async_remote_copy(
            src_ref=lines[k].at[block(zz)],
            dst_ref=lines[k].at[block(zz)],
            send_sem=s2s.at[k, 0],
            recv_sem=s2r.at[k, zz],
            device_id=device(hub_far, p),
            device_id_type=MESH,
        )

    def served(i):
        return (1 - upper) * (half - 2 - i) + upper * (half + 1 + i)

    def serve(k, i, zz):
        return pltpu.make_async_remote_copy(
            src_ref=fwds[k].at[i],
            dst_ref=sels[k],
            send_sem=s3s.at[k, i],
            recv_sem=s3r.at[k],
            device_id=device(zz, p),
            device_id_type=MESH,
        )

    def back(k, t, o):
        q = lax.rem(p + o, plane)
        return pltpu.make_async_remote_copy(
            src_ref=sels[k].at[t * plane + q],
            dst_ref=mate_ref.at[(t,) + piece(p, k)],
            send_sem=s4s.at[k, t, o],
            recv_sem=s4r.at[k, t, o],
            device_id=device(z, q),
            device_id_type=MESH,
        )

    def back_own(k, t):
        return pltpu.make_async_copy(
            sels[k].at[t * plane + p], mate_ref.at[(t,) + piece(p, k)], local4.at[k, t]
        )

    def each(count, start, body):
        def step(i, carry):
            body(i)
            return carry

        lax.fori_loop(start, count, step, 0)

    barrier = pltpu.get_barrier_semaphore()

    def greet_plane(o):
        pl.semaphore_signal(barrier, inc=1, device_id=device(z, lax.rem(p + o, plane)), device_id_type=MESH)

    def greet_line(o):
        pl.semaphore_signal(barrier, inc=1, device_id=device(lax.rem(z + o, nz), p), device_id_type=MESH)

    each(plane, 1, greet_plane)
    each(nz, 1, greet_line)
    pl.semaphore_wait(barrier, plane - 1 + nz - 1)

    def start_spread(k):
        spread_own(k).start()
        each(plane, 1, lambda o: spread(k, o).start())

    def send_line(k):
        spread_own(k).wait()
        each(plane, 1, lambda o: spread(k, o).wait_recv())
        to_hub(k, 0, hub_far).start()

        @pl.when(jnp.logical_not(is_hub))
        def _():
            to_hub(k, 1, hub_near).start()

    def send_back(k):
        for t in range(rounds):
            back_own(k, t).start()
            each(plane, 1, lambda o: back(k, t, o).start())

    def hub_step(k):
        each(nz, 1, lambda o: from_z(k, lax.rem(z + o, nz)).wait_recv())
        for i in range(half - 1):
            zz = served(i)

            def pick_far(j):
                want = partner_ref[j // plane, zz * plane + lax.rem(j, plane)]
                fwds[k][i, j] = lines[k][want]

            each(rounds * plane, 0, pick_far)
            serve(k, i, zz).start()

        def pick_own(j):
            want = partner_ref[j // plane, z * plane + lax.rem(j, plane)]
            sels[k][j] = lines[k][want]

        each(rounds * plane, 0, pick_own)
        send_back(k)

    def leaf_step(k):
        serve(k, 0, hub_near).wait_recv()
        send_back(k)

    start_spread(0)
    for s in range(chunks + 2):
        if s + 1 < chunks:
            start_spread(s + 1)
        if s < chunks:
            send_line(s)
        if 1 <= s <= chunks:
            pl.when(is_hub)(functools.partial(hub_step, s - 1))
        if s >= 2:
            pl.when(jnp.logical_not(is_hub))(functools.partial(leaf_step, s - 2))

    for k in range(chunks):
        for t in range(rounds):
            back_own(k, t).wait()
            each(plane, 1, lambda o: back(k, t, o).wait())
        each(plane, 1, lambda o: spread(k, o).wait_send())
        to_hub(k, 0, hub_far).wait_send()

        @pl.when(jnp.logical_not(is_hub))
        def _():
            to_hub(k, 1, hub_near).wait_send()

        @pl.when(is_hub)
        def _():
            for i in range(half - 1):
                serve(k, i, served(i)).wait_send()


def exchange(n_row, n_col, partner, own):
    rounds = partner.shape[0]
    nz, plane = n_row // 2, 2 * n_col
    leaves = nz // 2 - 1
    chunks = CHUNKS
    rows, width = own.shape[0] // 2 // chunks, own.shape[1] // n_col
    piece = (rows, width)
    dma = pltpu.SemaphoreType.DMA
    held = (nz + rounds * (leaves + 1)) * plane * rows * width * 4 * chunks
    return pl.pallas_call(
        functools.partial(exchange_kernel, n_row, n_col, rounds, chunks),
        out_shape=jax.ShapeDtypeStruct((rounds,) + own.shape, jnp.float32),
        in_specs=[pl.BlockSpec(memory_space=pltpu.SMEM), pl.BlockSpec(memory_space=pl.ANY)],
        out_specs=pl.BlockSpec(memory_space=pl.ANY),
        scratch_shapes=[pltpu.VMEM((nz * plane,) + piece, jnp.float32)] * chunks
        + [pltpu.VMEM((rounds * plane,) + piece, jnp.float32)] * chunks
        + [pltpu.VMEM((leaves, rounds * plane) + piece, jnp.float32)] * chunks
        + [
            dma((chunks, plane)),
            dma((chunks, plane)),
            dma((chunks, 2)),
            dma((chunks, nz)),
            dma((chunks, leaves)),
            dma((chunks,)),
            dma((chunks, rounds, plane)),
            dma((chunks, rounds, plane)),
            dma((chunks,)),
            dma((chunks, rounds)),
        ],
        compiler_params=pltpu.CompilerParams(
            collective_id=0, has_side_effects=True, vmem_limit_bytes=held + 4 * 2**20
        ),
        name="exchange",
    )(partner, own)


def local(blocks, eps_occ, eps_vir, partner):
    own = blocks[0]
    n_row, n_col = lax.axis_size("row"), lax.axis_size("col")
    orbital = lax.axis_index("row") * n_col + lax.axis_index("col")
    energy_own = lax.dynamic_index_in_dim(eps_occ, orbital, 0, keepdims=False)
    mates = exchange(n_row, n_col, partner, own)
    rounds = partner.shape[0]
    tamps = []
    dens = 0.0
    for t in range(rounds):
        mate = lax.dynamic_index_in_dim(partner[t], orbital, 0, keepdims=False)
        energy = lax.dynamic_index_in_dim(eps_occ, mate, 0, keepdims=False)
        pairs = jnp.dot(own, mates[t].T, precision=DOT, preferred_element_type=jnp.float32)
        denom = eps_vir[:, None] + eps_vir[None, :] - energy_own - energy
        amp = -pairs / denom
        tamp = 2.0 * amp - amp.T
        tamps.append(tamp)
        dens = dens + jnp.dot(amp, tamp.T, precision=DOT, preferred_element_type=jnp.float32)
    part = lax.psum_scatter(dens, "row", scatter_dimension=0, tiled=True)
    tile = lax.psum_scatter(part, "col", scatter_dimension=1, tiled=True)
    gamma = 0.0
    for t in range(rounds):
        gamma = gamma + jnp.dot(tamps[t], mates[t], precision=DOT, preferred_element_type=jnp.float32)
    return gamma[None], tile / jnp.float32(n_row * n_col)


def solution(mesh):
    in_specs = (P(("row", "col"), None, None), P(), P(), P())
    out_specs = (P(("row", "col"), None, None), P("row", "col"))
    return jax.shard_map(local, mesh=mesh, in_specs=in_specs, out_specs=out_specs, check_vma=False)
```

```python
import functools

import jax
import jax.numpy as jnp
from jax import lax
from jax.experimental import pallas as pl
from jax.experimental.pallas import tpu as pltpu
from jax.sharding import PartitionSpec as P

MESH = pl.DeviceIdType.MESH
CHUNKS = 12
DOT = lax.Precision.HIGH


def exchange_kernel(n_row, n_col, rounds, chunks, partner_ref, own_ref, mate_ref, *scratch):
    lines, sels, fwds = scratch[:chunks], scratch[chunks : 2 * chunks], scratch[2 * chunks : 3 * chunks]
    s1s, s1r, s2s, s2r, s3s, s3r, s4s, s4r, local1, local4 = scratch[3 * chunks :]
    nz, plane = n_row // 2, 2 * n_col
    half = nz // 2
    deep = own_ref.shape[0] // 2
    rows, width = deep // chunks, own_ref.shape[1] // n_col
    row, col = lax.axis_index("row"), lax.axis_index("col")
    z, y = row // 2, row % 2
    p = y * n_col + col
    upper = z // half
    hub_near = half - 1 + upper
    hub_far = half - upper
    is_hub = z == hub_near

    def device(zz, q):
        return (zz * 2 + q // n_col, q % n_col)

    def piece(q, k):
        return (
            pl.ds(pl.multiple_of(q // n_col * deep + k * rows, 8), rows),
            pl.ds(pl.multiple_of(q % n_col * width, 128), width),
        )

    def block(zz):
        return pl.ds(zz * plane, plane)

    def spread(k, o):
        q = lax.rem(p + o, plane)
        return pltpu.make_async_remote_copy(
            src_ref=own_ref.at[piece(q, k)],
            dst_ref=lines[k].at[z * plane + p],
            send_sem=s1s.at[k, o],
            recv_sem=s1r.at[k, o],
            device_id=device(z, q),
            device_id_type=MESH,
        )

    def spread_own(k):
        return pltpu.make_async_copy(own_ref.at[piece(p, k)], lines[k].at[z * plane + p], local1.at[k])

    def to_hub(k, slot, hub):
        return pltpu.make_async_remote_copy(
            src_ref=lines[k].at[block(z)],
            dst_ref=lines[k].at[block(z)],
            send_sem=s2s.at[k, slot],
            recv_sem=s2r.at[k, z],
            device_id=device(hub, p),
            device_id_type=MESH,
        )

    def from_z(k, zz):
        return pltpu.make_async_remote_copy(
            src_ref=lines[k].at[block(zz)],
            dst_ref=lines[k].at[block(zz)],
            send_sem=s2s.at[k, 0],
            recv_sem=s2r.at[k, zz],
            device_id=device(hub_far, p),
            device_id_type=MESH,
        )

    def served(i):
        return (1 - upper) * (half - 2 - i) + upper * (half + 1 + i)

    def serve(k, i, zz):
        return pltpu.make_async_remote_copy(
            src_ref=fwds[k].at[i],
            dst_ref=sels[k],
            send_sem=s3s.at[k, i],
            recv_sem=s3r.at[k],
            device_id=device(zz, p),
            device_id_type=MESH,
        )

    def back(k, t, o):
        q = lax.rem(p + o, plane)
        return pltpu.make_async_remote_copy(
            src_ref=sels[k].at[t * plane + q],
            dst_ref=mate_ref.at[(t,) + piece(p, k)],
            send_sem=s4s.at[k, t, o],
            recv_sem=s4r.at[k, t, o],
            device_id=device(z, q),
            device_id_type=MESH,
        )

    def back_own(k, t):
        return pltpu.make_async_copy(
            sels[k].at[t * plane + p], mate_ref.at[(t,) + piece(p, k)], local4.at[k, t]
        )

    def each(count, start, body):
        def step(i, carry):
            body(i)
            return carry

        lax.fori_loop(start, count, step, 0)

    barrier = pltpu.get_barrier_semaphore()

    def greet_plane(o):
        pl.semaphore_signal(barrier, inc=1, device_id=device(z, lax.rem(p + o, plane)), device_id_type=MESH)

    def greet_line(o):
        pl.semaphore_signal(barrier, inc=1, device_id=device(lax.rem(z + o, nz), p), device_id_type=MESH)

    each(plane, 1, greet_plane)
    each(nz, 1, greet_line)
    pl.semaphore_wait(barrier, plane - 1 + nz - 1)

    def start_spread(k):
        spread_own(k).start()
        each(plane, 1, lambda o: spread(k, o).start())

    def send_line(k):
        spread_own(k).wait()
        each(plane, 1, lambda o: spread(k, o).wait_recv())
        to_hub(k, 0, hub_far).start()

        @pl.when(jnp.logical_not(is_hub))
        def _():
            to_hub(k, 1, hub_near).start()

    def send_back(k):
        for t in range(rounds):
            back_own(k, t).start()
            each(plane, 1, lambda o: back(k, t, o).start())

    def hub_step(k):
        each(nz, 1, lambda o: from_z(k, lax.rem(z + o, nz)).wait_recv())
        for i in range(half - 1):
            zz = served(i)

            def pick_far(j):
                want = partner_ref[j // plane, zz * plane + lax.rem(j, plane)]
                fwds[k][i, j] = lines[k][want]

            each(rounds * plane, 0, pick_far)
            serve(k, i, zz).start()

        def pick_own(j):
            want = partner_ref[j // plane, z * plane + lax.rem(j, plane)]
            sels[k][j] = lines[k][want]

        each(rounds * plane, 0, pick_own)
        send_back(k)

    def leaf_step(k):
        serve(k, 0, hub_near).wait_recv()
        send_back(k)

    start_spread(0)
    for s in range(chunks + 2):
        if s + 1 < chunks:
            start_spread(s + 1)
        if s < chunks:
            send_line(s)
        if 1 <= s <= chunks:
            pl.when(is_hub)(functools.partial(hub_step, s - 1))
        if s >= 2:
            pl.when(jnp.logical_not(is_hub))(functools.partial(leaf_step, s - 2))

    for k in range(chunks):
        for t in range(rounds):
            back_own(k, t).wait()
            each(plane, 1, lambda o: back(k, t, o).wait())
        each(plane, 1, lambda o: spread(k, o).wait_send())
        to_hub(k, 0, hub_far).wait_send()

        @pl.when(jnp.logical_not(is_hub))
        def _():
            to_hub(k, 1, hub_near).wait_send()

        @pl.when(is_hub)
        def _():
            for i in range(half - 1):
                serve(k, i, served(i)).wait_send()


def exchange(n_row, n_col, partner, own):
    rounds = partner.shape[0]
    nz, plane = n_row // 2, 2 * n_col
    leaves = nz // 2 - 1
    chunks = CHUNKS
    rows, width = own.shape[0] // 2 // chunks, own.shape[1] // n_col
    piece = (rows, width)
    dma = pltpu.SemaphoreType.DMA
    held = (nz + rounds * (leaves + 1)) * plane * rows * width * 4 * chunks
    return pl.pallas_call(
        functools.partial(exchange_kernel, n_row, n_col, rounds, chunks),
        out_shape=jax.ShapeDtypeStruct((rounds,) + own.shape, jnp.float32),
        in_specs=[pl.BlockSpec(memory_space=pltpu.SMEM), pl.BlockSpec(memory_space=pl.ANY)],
        out_specs=pl.BlockSpec(memory_space=pl.ANY),
        scratch_shapes=[pltpu.VMEM((nz * plane,) + piece, jnp.float32)] * chunks
        + [pltpu.VMEM((rounds * plane,) + piece, jnp.float32)] * chunks
        + [pltpu.VMEM((leaves, rounds * plane) + piece, jnp.float32)] * chunks
        + [
            dma((chunks, plane)),
            dma((chunks, plane)),
            dma((chunks, 2)),
            dma((chunks, nz)),
            dma((chunks, leaves)),
            dma((chunks,)),
            dma((chunks, rounds, plane)),
            dma((chunks, rounds, plane)),
            dma((chunks,)),
            dma((chunks, rounds)),
        ],
        compiler_params=pltpu.CompilerParams(
            collective_id=0, has_side_effects=True, vmem_limit_bytes=held + 4 * 2**20
        ),
        name="exchange",
    )(partner, own)


def reduce_kernel(n_row, n_col, own_ref, out_ref, landed, total, final, as_, ar, bs, br):
    nz, plane = n_row // 2, 2 * n_col
    row, col = lax.axis_index("row"), lax.axis_index("col")
    z, y = row // 2, row % 2
    p = y * n_col + col

    def device(zz, q):
        return (zz * 2 + q // n_col, q % n_col)

    def each(count, body):
        def step(i, carry):
            body(i)
            return carry

        lax.fori_loop(1, count, step, 0)

    def in_plane(o):
        q = lax.rem(p + o, plane)
        return pltpu.make_async_remote_copy(
            src_ref=own_ref.at[q],
            dst_ref=landed.at[o],
            send_sem=as_.at[o],
            recv_sem=ar.at[o],
            device_id=device(z, q),
            device_id_type=MESH,
        )

    def in_line(o):
        zz = lax.rem(z + o, nz)
        return pltpu.make_async_remote_copy(
            src_ref=total.at[zz],
            dst_ref=final.at[o],
            send_sem=bs.at[o],
            recv_sem=br.at[o],
            device_id=device(zz, p),
            device_id_type=MESH,
        )

    barrier = pltpu.get_barrier_semaphore()

    def greet_plane(o):
        pl.semaphore_signal(barrier, inc=1, device_id=device(z, lax.rem(p + o, plane)), device_id_type=MESH)

    def greet_line(o):
        pl.semaphore_signal(barrier, inc=1, device_id=device(lax.rem(z + o, nz), p), device_id_type=MESH)

    each(plane, greet_plane)
    each(nz, greet_line)
    pl.semaphore_wait(barrier, plane - 1 + nz - 1)
    each(plane, lambda o: in_plane(o).start())
    total[...] = own_ref[p]

    def add_plane(o):
        in_plane(o).wait_recv()
        total[...] += landed[o]

    each(plane, add_plane)
    each(nz, lambda o: in_line(o).start())
    final[0] = total[z]

    def add_line(o):
        in_line(o).wait_recv()
        final[0] += final[o]

    each(nz, add_line)
    out_ref[...] = final[0] / (n_row * n_col)
    each(plane, lambda o: in_plane(o).wait_send())
    each(nz, lambda o: in_line(o).wait_send())


def reduce_density(n_row, n_col, dens):
    nz, plane = n_row // 2, 2 * n_col
    tile = (dens.shape[0] // n_row, dens.shape[1] // n_col)
    pieces = dens.reshape(nz, 2, tile[0], n_col, tile[1]).transpose(1, 3, 0, 2, 4).reshape((plane, nz) + tile)
    dma = pltpu.SemaphoreType.DMA
    return pl.pallas_call(
        functools.partial(reduce_kernel, n_row, n_col),
        out_shape=jax.ShapeDtypeStruct(tile, jnp.float32),
        in_specs=[pl.BlockSpec(memory_space=pltpu.VMEM)],
        out_specs=pl.BlockSpec(memory_space=pltpu.VMEM),
        scratch_shapes=[
            pltpu.VMEM((plane, nz) + tile, jnp.float32),
            pltpu.VMEM((nz,) + tile, jnp.float32),
            pltpu.VMEM((nz,) + tile, jnp.float32),
            dma((plane,)),
            dma((plane,)),
            dma((nz,)),
            dma((nz,)),
        ],
        compiler_params=pltpu.CompilerParams(
            collective_id=1, has_side_effects=True, vmem_limit_bytes=16 * 2**20
        ),
        name="reduce_density",
    )(pieces)


def local(blocks, eps_occ, eps_vir, partner):
    own = blocks[0]
    n_row, n_col = lax.axis_size("row"), lax.axis_size("col")
    orbital = lax.axis_index("row") * n_col + lax.axis_index("col")
    energy_own = lax.dynamic_index_in_dim(eps_occ, orbital, 0, keepdims=False)
    mates = exchange(n_row, n_col, partner, own)
    rounds = partner.shape[0]
    vir = own.shape[0]
    stacked = mates.reshape(rounds * vir, own.shape[1])
    pairs = jnp.dot(own, stacked.T, precision=DOT, preferred_element_type=jnp.float32)
    amps, tamps = [], []
    for t in range(rounds):
        mate = lax.dynamic_index_in_dim(partner[t], orbital, 0, keepdims=False)
        energy = lax.dynamic_index_in_dim(eps_occ, mate, 0, keepdims=False)
        denom = eps_vir[:, None] + eps_vir[None, :] - energy_own - energy
        amp = -pairs[:, t * vir : (t + 1) * vir] / denom
        amps.append(amp)
        tamps.append(2.0 * amp - amp.T)
    amps, tamps = jnp.concatenate(amps, axis=1), jnp.concatenate(tamps, axis=1)
    dens = jnp.dot(amps, tamps.T, precision=DOT, preferred_element_type=jnp.float32)
    tile = reduce_density(n_row, n_col, dens)
    gamma = jnp.dot(tamps, stacked, precision=DOT, preferred_element_type=jnp.float32)
    return gamma[None], tile


def solution(mesh):
    in_specs = (P(("row", "col"), None, None), P(), P(), P())
    out_specs = (P(("row", "col"), None, None), P("row", "col"))
    return jax.shard_map(local, mesh=mesh, in_specs=in_specs, out_specs=out_specs, check_vma=False)
```

```python
import functools

import jax
import jax.numpy as jnp
from jax import lax
from jax.experimental import pallas as pl
from jax.experimental.pallas import tpu as pltpu
from jax.sharding import PartitionSpec as P

MESH = pl.DeviceIdType.MESH
CHUNKS = 24
SEMAPHORES = 2400
AHEAD, HUB_LAG, LEAF_LAG = 1, 1, 2
COLUMNS = 256
DOT = lax.Precision.HIGH


def exchange_kernel(n_row, n_col, rounds, chunks, partner_ref, eps_ref, own_ref, mate_ref, energy_ref, *scratch):
    lines, sels, fwds = scratch[:chunks], scratch[chunks : 2 * chunks], scratch[2 * chunks : 3 * chunks]
    s1s, s1r, s2s, s2r, s3s, s3r, s4s, s4r, local1, local4 = scratch[3 * chunks :]
    nz, plane = n_row // 2, 2 * n_col
    half = nz // 2
    deep = own_ref.shape[0] // 2
    rows, width = deep // chunks, own_ref.shape[1] // n_col
    row, col = lax.axis_index("row"), lax.axis_index("col")
    z, y = row // 2, row % 2
    p = y * n_col + col
    upper = z // half
    hub_near = half - 1 + upper
    hub_far = half - upper
    is_hub = z == hub_near
    orbital = z * plane + p
    energy_ref[0] = eps_ref[orbital]
    for t in range(rounds):
        energy_ref[t + 1] = eps_ref[partner_ref[t, orbital]]

    def device(zz, q):
        return (zz * 2 + q // n_col, q % n_col)

    def piece(q, k):
        return (
            pl.ds(pl.multiple_of(q // n_col * deep + k * rows, 8), rows),
            pl.ds(pl.multiple_of(q % n_col * width, 128), width),
        )

    def block(zz):
        return pl.ds(zz * plane, plane)

    def spread(k, o):
        q = lax.rem(p + o, plane)
        return pltpu.make_async_remote_copy(
            src_ref=own_ref.at[piece(q, k)],
            dst_ref=lines[k].at[z * plane + p],
            send_sem=s1s.at[k, o],
            recv_sem=s1r.at[k, o],
            device_id=device(z, q),
            device_id_type=MESH,
        )

    def spread_own(k):
        return pltpu.make_async_copy(own_ref.at[piece(p, k)], lines[k].at[z * plane + p], local1.at[k])

    def to_hub(k, slot, hub):
        return pltpu.make_async_remote_copy(
            src_ref=lines[k].at[block(z)],
            dst_ref=lines[k].at[block(z)],
            send_sem=s2s.at[k, slot],
            recv_sem=s2r.at[k, z],
            device_id=device(hub, p),
            device_id_type=MESH,
        )

    def from_z(k, zz):
        return pltpu.make_async_remote_copy(
            src_ref=lines[k].at[block(zz)],
            dst_ref=lines[k].at[block(zz)],
            send_sem=s2s.at[k, 0],
            recv_sem=s2r.at[k, zz],
            device_id=device(hub_far, p),
            device_id_type=MESH,
        )

    def served(i):
        return (1 - upper) * (half - 2 - i) + upper * (half + 1 + i)

    def serve(k, i, zz):
        return pltpu.make_async_remote_copy(
            src_ref=fwds[k].at[i],
            dst_ref=sels[k],
            send_sem=s3s.at[k, i],
            recv_sem=s3r.at[k],
            device_id=device(zz, p),
            device_id_type=MESH,
        )

    def back(k, t, o):
        q = lax.rem(p + o, plane)
        return pltpu.make_async_remote_copy(
            src_ref=sels[k].at[t * plane + q],
            dst_ref=mate_ref.at[(t,) + piece(p, k)],
            send_sem=s4s.at[k, t, o],
            recv_sem=s4r.at[k, t, o],
            device_id=device(z, q),
            device_id_type=MESH,
        )

    def back_own(k, t):
        return pltpu.make_async_copy(
            sels[k].at[t * plane + p], mate_ref.at[(t,) + piece(p, k)], local4.at[k, t]
        )

    def each(count, start, body):
        def step(i, carry):
            body(i)
            return carry

        lax.fori_loop(start, count, step, 0)

    barrier = pltpu.get_barrier_semaphore()

    def greet_plane(o):
        pl.semaphore_signal(barrier, inc=1, device_id=device(z, lax.rem(p + o, plane)), device_id_type=MESH)

    def greet_line(o):
        pl.semaphore_signal(barrier, inc=1, device_id=device(lax.rem(z + o, nz), p), device_id_type=MESH)

    each(plane, 1, greet_plane)
    each(nz, 1, greet_line)
    pl.semaphore_wait(barrier, plane - 1 + nz - 1)

    def start_spread(k):
        spread_own(k).start()
        each(plane, 1, lambda o: spread(k, o).start())

    def send_line(k):
        spread_own(k).wait()
        each(plane, 1, lambda o: spread(k, o).wait_recv())
        to_hub(k, 0, hub_far).start()

        @pl.when(jnp.logical_not(is_hub))
        def _():
            to_hub(k, 1, hub_near).start()

    def send_back(k):
        for t in range(rounds):
            back_own(k, t).start()
            each(plane, 1, lambda o: back(k, t, o).start())

    def hub_step(k):
        each(nz, 1, lambda o: from_z(k, lax.rem(z + o, nz)).wait_recv())
        for i in range(half - 1):
            zz = served(i)

            def pick_far(j):
                want = partner_ref[j // plane, zz * plane + lax.rem(j, plane)]
                fwds[k][i, j] = lines[k][want]

            each(rounds * plane, 0, pick_far)
            serve(k, i, zz).start()

        def pick_own(j):
            want = partner_ref[j // plane, z * plane + lax.rem(j, plane)]
            sels[k][j] = lines[k][want]

        each(rounds * plane, 0, pick_own)
        send_back(k)

    def leaf_step(k):
        serve(k, 0, hub_near).wait_recv()
        send_back(k)

    for k in range(min(AHEAD, chunks)):
        start_spread(k)
    for s in range(chunks + LEAF_LAG):
        if s + AHEAD < chunks:
            start_spread(s + AHEAD)
        if s < chunks:
            send_line(s)
        if HUB_LAG <= s < chunks + HUB_LAG:
            pl.when(is_hub)(functools.partial(hub_step, s - HUB_LAG))
        if s >= LEAF_LAG:
            pl.when(jnp.logical_not(is_hub))(functools.partial(leaf_step, s - LEAF_LAG))

    for k in range(chunks):
        for t in range(rounds):
            back_own(k, t).wait()
            each(plane, 1, lambda o: back(k, t, o).wait())
        each(plane, 1, lambda o: spread(k, o).wait_send())
        to_hub(k, 0, hub_far).wait_send()

        @pl.when(jnp.logical_not(is_hub))
        def _():
            to_hub(k, 1, hub_near).wait_send()

        @pl.when(is_hub)
        def _():
            for i in range(half - 1):
                serve(k, i, served(i)).wait_send()


def exchange(n_row, n_col, partner, eps_occ, own):
    rounds = partner.shape[0]
    nz, plane = n_row // 2, 2 * n_col
    leaves = nz // 2 - 1
    chunks = CHUNKS
    while chunks % 2 == 0 and chunks * plane * (2 + 2 * rounds) > SEMAPHORES:
        chunks //= 2
    rows, width = own.shape[0] // 2 // chunks, own.shape[1] // n_col
    piece = (rows, width)
    dma = pltpu.SemaphoreType.DMA
    held = (nz + rounds * (leaves + 1)) * plane * rows * width * 4 * chunks
    return pl.pallas_call(
        functools.partial(exchange_kernel, n_row, n_col, rounds, chunks),
        out_shape=(
            jax.ShapeDtypeStruct((rounds,) + own.shape, jnp.float32),
            jax.ShapeDtypeStruct((rounds + 1,), jnp.float32),
        ),
        in_specs=[pl.BlockSpec(memory_space=pltpu.SMEM)] * 2 + [pl.BlockSpec(memory_space=pl.ANY)],
        out_specs=(pl.BlockSpec(memory_space=pl.ANY), pl.BlockSpec(memory_space=pltpu.SMEM)),
        scratch_shapes=[pltpu.VMEM((nz * plane,) + piece, jnp.float32)] * chunks
        + [pltpu.VMEM((rounds * plane,) + piece, jnp.float32)] * chunks
        + [pltpu.VMEM((leaves, rounds * plane) + piece, jnp.float32)] * chunks
        + [
            dma((chunks, plane)),
            dma((chunks, plane)),
            dma((chunks, 2)),
            dma((chunks, nz)),
            dma((chunks, leaves)),
            dma((chunks,)),
            dma((chunks, rounds, plane)),
            dma((chunks, rounds, plane)),
            dma((chunks,)),
            dma((chunks, rounds)),
        ],
        compiler_params=pltpu.CompilerParams(
            collective_id=0, has_side_effects=True, vmem_limit_bytes=held + 4 * 2**20
        ),
        name="exchange",
    )(partner, eps_occ, own)


def two_parts(value):
    high = value.astype(jnp.bfloat16)
    return high, (value - high.astype(jnp.float32)).astype(jnp.bfloat16)


def reduce_kernel(
    n_row, n_col, own_ref, tamp_ref, mate_ref, out_ref, gamma_ref, landed, total, final, high, low, as_, ar, bs, br
):
    nz, plane = n_row // 2, 2 * n_col
    row, col = lax.axis_index("row"), lax.axis_index("col")
    z, y = row // 2, row % 2
    p = y * n_col + col

    def device(zz, q):
        return (zz * 2 + q // n_col, q % n_col)

    def each(count, body, start=1):
        def step(i, carry):
            body(i)
            return carry

        lax.fori_loop(start, count, step, 0)

    def in_plane(o):
        q = lax.rem(p + o, plane)
        return pltpu.make_async_remote_copy(
            src_ref=own_ref.at[q],
            dst_ref=landed.at[o],
            send_sem=as_.at[o],
            recv_sem=ar.at[o],
            device_id=device(z, q),
            device_id_type=MESH,
        )

    def in_line(o):
        zz = lax.rem(z + o, nz)
        return pltpu.make_async_remote_copy(
            src_ref=total.at[zz],
            dst_ref=final.at[o],
            send_sem=bs.at[o],
            recv_sem=br.at[o],
            device_id=device(zz, p),
            device_id_type=MESH,
        )

    barrier = pltpu.get_barrier_semaphore()

    def greet_plane(o):
        pl.semaphore_signal(barrier, inc=1, device_id=device(z, lax.rem(p + o, plane)), device_id_type=MESH)

    def greet_line(o):
        pl.semaphore_signal(barrier, inc=1, device_id=device(lax.rem(z + o, nz), p), device_id_type=MESH)

    each(plane, greet_plane)
    each(nz, greet_line)
    pl.semaphore_wait(barrier, plane - 1 + nz - 1)
    each(plane, lambda o: in_plane(o).start())
    total[...] = own_ref[p]
    split = gamma_ref.shape[1] // COLUMNS
    early = split * 3 // 4
    high[...], low[...] = two_parts(tamp_ref[...])

    def gamma_part(i):
        columns = pl.ds(pl.multiple_of(i * COLUMNS, COLUMNS), COLUMNS)
        mate_high, mate_low = two_parts(mate_ref[:, columns])
        part = jnp.dot(low[...], mate_high, preferred_element_type=jnp.float32)
        part += jnp.dot(high[...], mate_low, preferred_element_type=jnp.float32)
        part += jnp.dot(high[...], mate_high, preferred_element_type=jnp.float32)
        gamma_ref[:, columns] = part

    each(early, gamma_part, 0)

    def add_plane(o):
        in_plane(o).wait_recv()
        total[...] += landed[o]

    each(plane, add_plane)
    each(nz, lambda o: in_line(o).start())
    final[0] = total[z]
    each(split, gamma_part, early)

    def add_line(o):
        in_line(o).wait_recv()
        final[0] += final[o]

    each(nz, add_line)
    out_ref[...] = final[0] / (n_row * n_col)
    each(plane, lambda o: in_plane(o).wait_send())
    each(nz, lambda o: in_line(o).wait_send())


def reduce_density(n_row, n_col, dens, tamps, stacked):
    nz, plane = n_row // 2, 2 * n_col
    tile = (dens.shape[0] // n_row, dens.shape[1] // n_col)
    pieces = dens.reshape(nz, 2, tile[0], n_col, tile[1]).transpose(1, 3, 0, 2, 4).reshape((plane, nz) + tile)
    dma = pltpu.SemaphoreType.DMA
    return pl.pallas_call(
        functools.partial(reduce_kernel, n_row, n_col),
        out_shape=(
            jax.ShapeDtypeStruct(tile, jnp.float32),
            jax.ShapeDtypeStruct((tamps.shape[0], stacked.shape[1]), jnp.float32),
        ),
        in_specs=[pl.BlockSpec(memory_space=pltpu.VMEM)] * 3,
        out_specs=(pl.BlockSpec(memory_space=pltpu.VMEM),) * 2,
        scratch_shapes=[
            pltpu.VMEM((plane, nz) + tile, jnp.float32),
            pltpu.VMEM((nz,) + tile, jnp.float32),
            pltpu.VMEM((nz,) + tile, jnp.float32),
            pltpu.VMEM(tamps.shape, jnp.bfloat16),
            pltpu.VMEM(tamps.shape, jnp.bfloat16),
            dma((plane,)),
            dma((plane,)),
            dma((nz,)),
            dma((nz,)),
        ],
        compiler_params=pltpu.CompilerParams(
            collective_id=1, has_side_effects=True, vmem_limit_bytes=20 * 2**20
        ),
        name="reduce_density",
    )(pieces, tamps, stacked)


def local(blocks, eps_occ, eps_vir, partner):
    own = blocks[0]
    n_row, n_col = lax.axis_size("row"), lax.axis_size("col")
    mates, energies = exchange(n_row, n_col, partner, eps_occ, own)
    rounds = partner.shape[0]
    vir = own.shape[0]
    stacked = mates.reshape(rounds * vir, own.shape[1])
    pairs = jnp.dot(own, stacked.T, precision=DOT, preferred_element_type=jnp.float32)
    amps, tamps = [], []
    for t in range(rounds):
        denom = eps_vir[:, None] + eps_vir[None, :] - energies[0] - energies[t + 1]
        amp = -pairs[:, t * vir : (t + 1) * vir] / denom
        amps.append(amp)
        tamps.append(2.0 * amp - amp.T)
    amps, tamps = jnp.concatenate(amps, axis=1), jnp.concatenate(tamps, axis=1)
    dens = jnp.dot(amps, tamps.T, precision=DOT, preferred_element_type=jnp.float32)
    tile, gamma = reduce_density(n_row, n_col, dens, tamps, stacked)
    return gamma[None], tile


def solution(mesh):
    in_specs = (P(("row", "col"), None, None), P(), P(), P())
    out_specs = (P(("row", "col"), None, None), P("row", "col"))
    return jax.shard_map(local, mesh=mesh, in_specs=in_specs, out_specs=out_specs, check_vma=False)
```
